32 devices in a mesh: dp: 4 (over y, x), tensor: 8 (over z, core).
Axes of the slice: x: 2, y: 2, z: 4, core: 2. Of those that a mesh axis runs over, the one named last changes fastest.
Arguments:
- inputs: bfloat16 [1024, 28672], P('dp', 'tensor'), may hold values from -0.1875 to 0.1875
- output_gradient: bfloat16 [1024, 8192], P('dp', 'tensor'), may hold values from -6 to 6
- frozen: bfloat16 [8192, 28672], P('dp', 'tensor'), may hold values from -0.5905695 to 0.5905695
- adapter_down_factor: bfloat16 [64, 28672], P(None, 'tensor'), may hold values from -0.03125 to 0.03125
- adapter_up_factor: bfloat16 [8192, 64], P('dp'), may hold values from -0.3125 to 0.3125
- magnitude: float32 [8192], P('dp'), may hold values from 0.5 to 2
Outputs:
- input_gradient_rows: bfloat16 [1024, 28672], P('dp', 'tensor')
- adapter_down_gradient: float32 [64, 28672], P(None, 'tensor')
- adapter_up_gradient: float32 [8192, 64], P('dp')
- magnitude_gradient: float32 [8192], P('dp')
The draws below stay inside these ranges and needn't reach their ends.
All inputs are finite; a program needn't handle non-finite values.
Results may differ from the reference program's by a relative error of at most 0.0057.
Values may be sent and summed in bfloat16 or wider, within the bound.
A program may use at most 192 MiB of HBM per device.

```python
import math
import jax
import jax.numpy as jnp
from jax import lax

OUTPUT_WIDTH = 8192
INPUT_WIDTH = 28672
ADAPTER_RANK = 64
TOKENS = 1024
N_TENSOR = 8


def draw_frozen(key, part):
    base_key = jax.random.fold_in(key, 11)
    row_key, col_key, noise_key = jax.random.split(base_key, 3)
    row_scale = jnp.exp(jax.random.uniform(row_key, (OUTPUT_WIDTH, 1), jnp.float32) * math.log(10.0))
    col_scale = jnp.exp(jax.random.uniform(col_key, (1, INPUT_WIDTH), jnp.float32) * math.log(10.0))
    position = jnp.arange(INPUT_WIDTH, dtype=jnp.float32)[None, :] / INPUT_WIDTH
    noise = jax.random.truncated_normal(noise_key, -4.0, 4.0, (OUTPUT_WIDTH, INPUT_WIDTH), jnp.float32)
    trend = jnp.exp(position * math.log(3.0))
    values = noise * row_scale * col_scale * trend / (16.0 * math.sqrt(INPUT_WIDTH))
    return values.astype(jnp.bfloat16)


def levels(key, extent, cuts, least, top_value):
    loudness, own = 1.0, jax.random.fold_in(key, 6)
    for dim, shards_of in cuts:
        heights = jnp.exp(jax.random.uniform(jax.random.fold_in(own, dim), (shards_of,), jnp.float32, least / len(cuts), top_value / len(cuts)))
        loudness = loudness * jnp.repeat(heights, extent[dim] // shards_of).reshape([-1 if axis == dim else 1 for axis in range(len(extent))])
    return loudness


def normal_values(key, shape, deviation, most, cuts=(), kind=jnp.bfloat16):
    drawn = deviation * jax.random.normal(key, shape, jnp.float32)
    if cuts:
        drawn = drawn * levels(key, shape, cuts, -0.22, 0.18)
    return jnp.clip(drawn, -most, most).astype(kind)


def setup_inputs(seed: int = 0) -> dict:
    key_list = jax.random.split(jax.random.key(seed), 7)
    return {
        "inputs": normal_values(key_list[0], (TOKENS, INPUT_WIDTH), (TOKENS ** -0.5), 0.1875, ((0, 4), (1, 8))),
        "output_gradient": normal_values(key_list[1], (TOKENS, OUTPUT_WIDTH), 1.0, 6.0, ((0, 4), (1, 8))),
        "frozen": draw_frozen(jax.random.fold_in(key_list[6], 71), 0),
        "adapter_down_factor": normal_values(key_list[3], (ADAPTER_RANK, INPUT_WIDTH), INPUT_WIDTH ** -0.5, 0.03125, ((1, 8),)),
        "adapter_up_factor": normal_values(key_list[4], (OUTPUT_WIDTH, ADAPTER_RANK), 0.05, 0.3125, ((0, 4),)),
        "magnitude": jnp.clip(jnp.exp(math.log(2.0) - 1.3862944 * jax.random.uniform(key_list[5], (OUTPUT_WIDTH,), jnp.float32) ** levels(key_list[5], (OUTPUT_WIDTH,), ((0, 4),), -0.2, 0.2)), 0.5, 2.0),
    }


adapter_scale = 2.0
epsilon = 1e-06

def reference(inputs, output_gradient, frozen, adapter_down_factor, adapter_up_factor, magnitude):
    block_column_count = INPUT_WIDTH // N_TENSOR
    offsets = jnp.arange(N_TENSOR, dtype=jnp.int32) * block_column_count

    def merged_block(column_start):
        down_factor_block = lax.dynamic_slice_in_dim(adapter_down_factor, column_start, block_column_count, 1)
        weight_block_slice = lax.dynamic_slice_in_dim(frozen, column_start, block_column_count, 1)
        return weight_block_slice.astype(jnp.float32) + adapter_scale * jnp.dot(adapter_up_factor, down_factor_block, preferred_element_type=jnp.float32)

    def product_block(column_start):
        x_block = lax.dynamic_slice_in_dim(inputs, column_start, block_column_count, 1)
        return lax.dot_general(output_gradient, x_block, (((0,), (0,)), ((), ())), preferred_element_type=jnp.float32)

    def gather_stats(state_pair, column_start):
        squares, gradient_row_sums = state_pair
        combined_weight = merged_block(column_start)
        product = product_block(column_start)
        return ((squares + lax.optimization_barrier(jnp.sum(combined_weight * combined_weight, axis=1)), gradient_row_sums + lax.optimization_barrier(jnp.sum(product * combined_weight, axis=1))), None)
    initial = (jnp.zeros((OUTPUT_WIDTH,), jnp.float32), jnp.zeros((OUTPUT_WIDTH,), jnp.float32))
    (squares, gradient_row_sums), unused = lax.scan(gather_stats, initial, offsets)
    weight_row_norm = jnp.sqrt(squares + epsilon)
    col_scale = magnitude / weight_row_norm
    scaled_grad = (output_gradient.astype(jnp.float32) * col_scale[None, :]).astype(jnp.bfloat16)

    def make_grads(running, column_start):
        combined_weight = merged_block(column_start)
        product = product_block(column_start)
        combined_weight_gradient = col_scale[:, None] * product
        down_factor_gradient = adapter_scale * jnp.dot(adapter_up_factor.astype(jnp.float32).T, combined_weight_gradient, precision=lax.Precision.HIGHEST)
        down_factor_block = lax.dynamic_slice_in_dim(adapter_down_factor, column_start, block_column_count, 1)
        up_factor_piece = adapter_scale * jnp.dot(combined_weight_gradient, down_factor_block.astype(jnp.float32).T, precision=lax.Precision.HIGHEST)
        x_grad = jnp.dot(scaled_grad, combined_weight.astype(jnp.bfloat16), preferred_element_type=jnp.float32).astype(jnp.bfloat16)
        return (running + up_factor_piece, (x_grad, down_factor_gradient))
    up_factor_gradient, (x_blocks, down_factor_blocks) = lax.scan(make_grads, jnp.zeros((OUTPUT_WIDTH, ADAPTER_RANK), jnp.float32), offsets)
    input_gradient_rows = jnp.transpose(x_blocks, (1, 0, 2)).reshape(TOKENS, INPUT_WIDTH)
    adapter_down_gradient = jnp.transpose(down_factor_blocks, (1, 0, 2)).reshape(ADAPTER_RANK, INPUT_WIDTH)
    return (input_gradient_rows, adapter_down_gradient, up_factor_gradient, gradient_row_sums / weight_row_norm)
```

```python
import jax
import jax.numpy as jnp
from jax import lax
from jax.sharding import PartitionSpec as P

adapter_scale = 2.0
epsilon = 1e-06
bf16, f32 = jnp.bfloat16, jnp.float32


def two_parts(value):
    high = value.astype(bf16)
    return high, (value - high.astype(f32)).astype(bf16)


def mm(a, b, ca, cb):
    return lax.dot_general(a, b, (((ca,), (cb,)), ((), ())), preferred_element_type=f32)


def local(inputs, output_gradient, frozen, down, up, magnitude):
    nd, nt = lax.axis_size("dp"), lax.axis_size("tensor")
    k = nt // nd
    tokens, columns = inputs.shape
    rank = down.shape[0]
    me = lax.axis_index("dp")
    same = [[m + k * q for q in range(nd)] for m in range(k)]
    near = [[k * q + m for m in range(k)] for q in range(nd)]
    part = lax.all_gather(output_gradient, "tensor", axis=0, axis_index_groups=same)
    part = lax.all_to_all(part, "dp", split_axis=0, concat_axis=0)
    grad = lax.all_gather(part, "tensor", axis=2, axis_index_groups=near, tiled=True)
    grad = grad.reshape(nd * tokens, -1)
    x_down = lax.psum(mm(inputs, down, 1, 1), "tensor")
    x_down = lax.all_gather(x_down, "dp", axis=0, tiled=True)
    all_inputs = lax.all_gather(inputs, "dp", axis=0, tiled=True)

    merged = frozen.astype(f32) + adapter_scale * mm(up, down, 1, 0)
    merged_b = merged.astype(bf16)
    squares = lax.psum(jnp.sum(merged * merged, axis=1), "tensor")
    norm = jnp.sqrt(squares + epsilon)
    scale = magnitude / norm
    scaled = (grad.astype(f32) * scale[None, :]).astype(bf16)

    blocks = [((me ^ s) * tokens) for s in range(nd)]

    def share(start):
        return mm(lax.dynamic_slice_in_dim(scaled, start, tokens, 0), merged_b, 1, 0)

    def swap(value, s):
        return lax.ppermute(value, "dp", [(i, i ^ s) for i in range(nd)])

    half = tokens // 2
    far = share(blocks[3]).astype(bf16)
    on_1 = share(blocks[1])
    on_2 = share(blocks[2])
    a1, b1 = swap(far[:half], 1), swap(far[half:], 2)
    a2, b2 = swap(on_1[:half].astype(bf16), 1), swap(on_2[half:].astype(bf16), 2)
    own = share(blocks[0])
    a3 = swap((on_2[:half] + a1.astype(f32)).astype(bf16), 2)
    b3 = swap((on_1[half:] + b1.astype(f32)).astype(bf16), 1)
    first = own[:half] + a2.astype(f32) + a3.astype(f32)
    second = own[half:] + b2.astype(f32) + b3.astype(f32)
    input_gradient_rows = jnp.concatenate([first, second], 0).astype(bf16)

    high, low = two_parts(scale[:, None] * up.astype(f32))
    both = mm(grad, jnp.concatenate([high, low], 1), 1, 0)
    g_up = lax.psum(both[:, :rank] + both[:, rank:], "dp")
    high, low = two_parts(g_up)
    both = mm(jnp.concatenate([high, low], 1), all_inputs, 0, 0)
    adapter_down_gradient = adapter_scale * (both[:rank] + both[rank:])
    high, low = two_parts(x_down)
    both = mm(grad, jnp.concatenate([high, low], 1), 0, 0)
    product_down = both[:, :rank] + both[:, rank:]
    adapter_up_gradient = adapter_scale * scale[:, None] * product_down
    y = mm(all_inputs, frozen, 1, 1)
    sums = lax.psum(jnp.sum(y * grad.astype(f32), axis=0), "tensor")
    sums = sums + adapter_scale * jnp.sum(up.astype(f32) * product_down, axis=1)
    return input_gradient_rows, adapter_down_gradient, adapter_up_gradient, sums / norm


def solution(mesh):
    placed = (
        P("dp", "tensor"),
        P("dp", "tensor"),
        P("dp", "tensor"),
        P(None, "tensor"),
        P("dp", None),
        P("dp"),
    )
    return jax.shard_map(
        local,
        mesh=mesh,
        in_specs=placed,
        out_specs=(P("dp", "tensor"), P(None, "tensor"), P("dp", None), P("dp")),
        check_vma=False,
    )
```

```python
import functools

import jax
import jax.numpy as jnp
from jax import lax
from jax.experimental import pallas as pl
from jax.experimental.pallas import tpu as pltpu
from jax.sharding import PartitionSpec as P

adapter_scale = 2.0
epsilon = 1e-06
bf16, f32 = jnp.bfloat16, jnp.float32
MESH = pl.DeviceIdType.MESH


def mm(a, b, ca, cb):
    return lax.dot_general(a, b, (((ca,), (cb,)), ((), ())), preferred_element_type=f32)


def kernel(
    nd, nt, n_local,
    x_ref, g_ref, w_ref, down_ref, up_ref, upt_ref, mag_ref,
    dx_ref, dg_ref, ug_ref, mg_ref,
    w, x, gz, grad, scaled, part, own, got, u_part, u, v, squares, sums,
    send, recv, local_sem,
):
    d, t = lax.axis_index("dp"), lax.axis_index("tensor")
    k = nt // nd
    q, m = t // k, t % k
    tokens, columns = x_ref.shape
    rows = w_ref.shape[0]
    nr = g_ref.shape[1]
    half = tokens // 2
    n_tile = 7
    width = columns // n_tile
    side = 256
    p1, p2, p3 = d + 1 - 2 * (d % 2), (d + 2) % nd, nd - 1 - d
    started, used = [], [0]

    def remote(src, dst, to):
        i = used[0]
        used[0] += 1
        copy = pltpu.make_async_remote_copy(
            src_ref=src, dst_ref=dst, send_sem=send.at[i], recv_sem=recv.at[i],
            device_id=to, device_id_type=MESH,
        )
        started.append(copy)
        copy.start()
        return copy

    def block(index, size=None, offset=0):
        return pl.ds(pl.multiple_of(index * tokens + offset, half), size or tokens)

    load_x = pltpu.make_async_copy(x_ref, x.at[block(d)], local_sem.at[0])
    load_x.start()
    load_g = pltpu.make_async_copy(g_ref, gz.at[q], local_sem.at[1])
    load_g.start()
    load_w = pltpu.make_async_copy(w_ref, w, local_sem.at[2])
    load_w.start()

    barrier = pltpu.get_barrier_semaphore()
    for peer in (p1, p2, p3):
        pl.semaphore_signal(barrier, inc=1, device_id=(peer, t), device_id_type=MESH)
    for o in range(1, nt):
        pl.semaphore_signal(barrier, inc=1, device_id=(d, (t + o) % nt), device_id_type=MESH)
    pl.semaphore_wait(barrier, nd - 1 + nt - 1)

    def share_out(slots):
        return [remote(slots.at[t], slots.at[t], (d, (t + o) % nt)) for o in range(1, nt)]

    x1 = remote(x_ref, x.at[block(d)], (p1, t))
    x2 = remote(x_ref, x.at[block(d)], (p2, t))
    gathered = [
        remote(g_ref, gz.at[q], (d, ((q + o) % nd) * k + m)) for o in range(1, nd)
    ]

    load_x.wait()
    u_part[t] = mm(down_ref[...], x[block(d)], 1, 1)
    u_sent = share_out(u_part)

    load_w.wait()

    @pl.loop(0, rows // side)
    def _(i):
        r = pl.ds(pl.multiple_of(i * side, side), side)
        total = jnp.zeros((side, 128), f32)
        for c in range(n_tile):
            cols = slice(c * width, (c + 1) * width)
            merged = w[r, cols].astype(f32) + adapter_scale * mm(up_ref[r, :], down_ref[:, cols], 1, 0)
            w[r, cols] = merged.astype(bf16)
            square = merged * merged
            for lane in range(0, width, 128):
                total = total + square[:, lane:lane + 128]
        squares[t, :, r] = jnp.sum(total.T, axis=0, keepdims=True)

    squares_sent = share_out(squares)

    load_g.wait()
    for copy in gathered:
        copy.wait_recv()
    moved = [
        remote(gz.at[p], grad.at[m, block(d)], (p, t)) for p in (p3, p1, p2)
    ]
    keep_g = pltpu.make_async_copy(gz.at[d], grad.at[m, block(d)], local_sem.at[3])
    keep_g.start()

    def near(source):
        return [
            remote(grad.at[m, block(source)], grad.at[m, block(source)], (d, q * k + (m + o) % k))
            for o in range(1, k)
        ]

    for copy in u_sent:
        copy.wait_recv()
    total = u_part[0]
    for i in range(1, nt):
        total = total + u_part[i]
    u[d] = total.astype(bf16)
    u_moved = [remote(u.at[d], u.at[d], (p, t)) for p in (p1, p2, p3)]

    for copy in squares_sent:
        copy.wait_recv()
    total = squares[0]
    for i in range(1, nt):
        total = total + squares[i]
    norm = jnp.sqrt(total + epsilon)
    scale = mag_ref[...] / norm

    keep_g.wait()
    swapped = {0: near(d)}
    x1.wait_recv()
    x2.wait_recv()
    for s, copy, p in zip((3, 1, 2), moved, (p3, p1, p2)):
        copy.wait_recv()
        swapped[s] = near(p)
    x3 = remote(x.at[block(p1, half)], x.at[block(p1, half)], (p2, t))
    x4 = remote(x.at[block(p2, half, half)], x.at[block(p2, half, half)], (p1, t))

    def share(s, p):
        for copy in swapped[s]:
            copy.wait_recv()
        at = block(p)
        for j in range(k):
            scaled[j, at] = (grad[j, at].astype(f32) * scale[:, j * nr:(j + 1) * nr]).astype(bf16)

        @pl.loop(0, n_tile)
        def _(i):
            cols = pl.ds(pl.multiple_of(i * width, width), width)
            acc = mm(scaled[0, at], w[0:nr, cols], 1, 0)
            for j in range(1, k):
                acc = acc + mm(scaled[j, at], w[j * nr:(j + 1) * nr, cols], 1, 0)
            if s:
                part[s - 1, :, cols] = acc.astype(bf16)
            else:
                own[:, cols] = acc

    low, high = pl.ds(0, half), pl.ds(half, half)
    share(3, p3)
    a1 = remote(part.at[2, low], got.at[0], (p1, t))
    b1 = remote(part.at[2, high], got.at[1], (p2, t))
    share(1, p1)
    a2 = remote(part.at[0, low], got.at[2], (p1, t))
    share(2, p2)
    b2 = remote(part.at[1, high], got.at[3], (p2, t))
    share(0, d)

    total = mm(upt_ref[:, 0:nr], scaled[0], 1, 1)
    for j in range(1, k):
        total = total + mm(upt_ref[:, j * nr:(j + 1) * nr], scaled[j], 1, 1)
    v[d] = total.astype(bf16)
    v_moved = [remote(v.at[d], v.at[d], (p, t)) for p in (p1, p2, p3)]

    def combine(copy, slot, index, at):
        copy.wait_recv()

        @pl.loop(0, n_tile)
        def _(i):
            cols = pl.ds(pl.multiple_of(i * width, width), width)
            part[index, at, cols] = (
                part[index, at, cols].astype(f32) + got[slot, :, cols].astype(f32)
            ).astype(bf16)

    x3.wait_recv()
    x4.wait_recv()

    def row_sums(j):
        @pl.loop(0, nr // side)
        def _(i):
            r = pl.ds(pl.multiple_of(j * nr + i * side, side), side)
            inner = pl.ds(pl.multiple_of(i * side, side), side)
            y = mm(x[...], w[r, :], 1, 1)
            sums[t, :, r] = jnp.sum(y * grad[j, :, inner].astype(f32), axis=0, keepdims=True)

    for j in range(k // 2):
        row_sums(j)
    combine(a1, 0, 1, low)
    a3 = remote(part.at[1, low], got.at[4], (p2, t))
    combine(b1, 1, 0, high)
    b3 = remote(part.at[0, high], got.at[5], (p1, t))
    for j in range(k // 2, k):
        row_sums(j)
    sums_sent = share_out(sums)

    for copy in u_moved:
        copy.wait_recv()
    for j in range(k):
        total = mm(u[0], grad[j, 0:tokens], 1, 0)
        for b in range(1, nd):
            total = total + mm(u[b], grad[j, b * tokens:(b + 1) * tokens], 1, 0)
        at = slice(j * nr, (j + 1) * nr)
        ug_ref[:, at] = adapter_scale * scale[:, at] * total

    for copy in v_moved:
        copy.wait_recv()
    total = v[0].astype(f32)
    for b in range(1, nd):
        total = total + v[b].astype(f32)
    v_all = total.astype(bf16)
    for c in range(n_tile):
        cols = slice(c * width, (c + 1) * width)
        dg_ref[:, cols] = adapter_scale * mm(v_all, x[:, cols], 1, 0)

    for copy in sums_sent:
        copy.wait_recv()
    total = sums[0]
    for i in range(1, nt):
        total = total + sums[i]
    mg_ref[...] = total / norm

    def finish(second, third, i2, i3, at):
        second.wait_recv()
        third.wait_recv()

        @pl.loop(0, n_tile)
        def _(i):
            cols = pl.ds(pl.multiple_of(i * width, width), width)
            dx_ref[at, cols] = (
                own[at, cols] + got[i2, :, cols].astype(f32) + got[i3, :, cols].astype(f32)
            ).astype(bf16)

    finish(a2, a3, 2, 4, low)
    finish(b2, b3, 3, 5, high)
    for copy in started:
        copy.wait_send()
    assert used[0] == n_local, used[0]


def local(inputs, output_gradient, frozen, down, up, magnitude):
    nd, nt = lax.axis_size("dp"), lax.axis_size("tensor")
    k = nt // nd
    tokens, columns = inputs.shape
    rows = frozen.shape[0]
    rank = down.shape[0]
    nr = output_gradient.shape[1]
    n_copies = 2 + (nd - 1) + 3 * (nt - 1) + 3 * 3 + nd * (k - 1) + 2 + 6
    anywhere = pl.BlockSpec(memory_space=pl.ANY)
    vmem = pl.BlockSpec(memory_space=pltpu.VMEM)
    half = tokens // 2
    dx, dg, ug, mg = pl.pallas_call(
        functools.partial(kernel, nd, nt, n_copies),
        out_shape=(
            jax.ShapeDtypeStruct((tokens, columns), bf16),
            jax.ShapeDtypeStruct((rank, columns), f32),
            jax.ShapeDtypeStruct((rank, rows), f32),
            jax.ShapeDtypeStruct((1, rows), f32),
        ),
        in_specs=[anywhere] * 3 + [vmem] * 4,
        out_specs=(vmem,) * 4,
        scratch_shapes=[
            pltpu.VMEM((rows, columns), bf16),
            pltpu.VMEM((nd * tokens, columns), bf16),
            pltpu.VMEM((nd, tokens, nr), bf16),
            pltpu.VMEM((k, nd * tokens, nr), bf16),
            pltpu.VMEM((k, nd * tokens, nr), bf16),
            pltpu.VMEM((3, tokens, columns), bf16),
            pltpu.VMEM((tokens, columns), f32),
            pltpu.VMEM((6, half, columns), bf16),
            pltpu.VMEM((nt, rank, tokens), f32),
            pltpu.VMEM((nd, rank, tokens), bf16),
            pltpu.VMEM((nd, rank, nd * tokens), bf16),
            pltpu.VMEM((nt, 1, rows), f32),
            pltpu.VMEM((nt, 1, rows), f32),
            pltpu.SemaphoreType.DMA((n_copies,)),
            pltpu.SemaphoreType.DMA((n_copies,)),
            pltpu.SemaphoreType.DMA((4,)),
        ],
        compiler_params=pltpu.CompilerParams(
            collective_id=0, has_side_effects=True, vmem_limit_bytes=62 * 1024 * 1024
        ),
    )(inputs, output_gradient, frozen, down, up, up.T, magnitude[None, :])
    return dx, dg, ug.T, mg[0]


def solution(mesh):
    placed = (
        P("dp", "tensor"),
        P("dp", "tensor"),
        P("dp", "tensor"),
        P(None, "tensor"),
        P("dp", None),
        P("dp"),
    )
    return jax.shard_map(
        local,
        mesh=mesh,
        in_specs=placed,
        out_specs=(P("dp", "tensor"), P(None, "tensor"), P("dp", None), P("dp")),
        check_vma=False,
    )
```

```python
import functools

import jax
import jax.numpy as jnp
from jax import lax
from jax.experimental import pallas as pl
from jax.experimental.pallas import tpu as pltpu
from jax.sharding import PartitionSpec as P

adapter_scale = 2.0
epsilon = 1e-06
bf16, f32 = jnp.bfloat16, jnp.float32
MESH = pl.DeviceIdType.MESH


def mm(a, b, ca, cb):
    return lax.dot_general(a, b, (((ca,), (cb,)), ((), ())), preferred_element_type=f32)


def kernel(
    nd, nt, n_local,
    x_ref, g_ref, w_ref, down_ref, up_ref, upt_ref, mag_ref,
    dx_ref, dg_ref, ug_ref, mg_ref,
    w, x, gz, grad, scaled, part, own, got, u_part, u, v, v_all, squares, sums,
    send, recv, local_sem,
):
    d, t = lax.axis_index("dp"), lax.axis_index("tensor")
    k = nt // nd
    q, m = t // k, t % k
    tokens, columns = x_ref.shape
    rows = w_ref.shape[0]
    nr = g_ref.shape[1]
    half = tokens // 2
    n_tile = 7
    width = columns // n_tile
    side = 256
    p1, p2, p3 = d + 1 - 2 * (d % 2), (d + 2) % nd, nd - 1 - d
    started, used = [], [0]

    def remote(src, dst, to):
        i = used[0]
        used[0] += 1
        copy = pltpu.make_async_remote_copy(
            src_ref=src, dst_ref=dst, send_sem=send.at[i], recv_sem=recv.at[i],
            device_id=to, device_id_type=MESH,
        )
        started.append(copy)
        copy.start()
        return copy

    def block(index, size=None, offset=0):
        return pl.ds(pl.multiple_of(index * tokens + offset, half), size or tokens)

    load_x = pltpu.make_async_copy(x_ref, x.at[block(d)], local_sem.at[0])
    load_x.start()
    load_g = pltpu.make_async_copy(g_ref, gz.at[q], local_sem.at[1])
    load_g.start()
    load_w = pltpu.make_async_copy(w_ref, w, local_sem.at[2])
    load_w.start()

    barrier = pltpu.get_barrier_semaphore()
    for peer in (p1, p2, p3):
        pl.semaphore_signal(barrier, inc=1, device_id=(peer, t), device_id_type=MESH)
    for o in range(1, nt):
        pl.semaphore_signal(barrier, inc=1, device_id=(d, (t + o) % nt), device_id_type=MESH)
    pl.semaphore_wait(barrier, nd - 1 + nt - 1)

    def share_out(slots):
        return [remote(slots.at[t], slots.at[t], (d, (t + o) % nt)) for o in range(1, nt)]

    x1 = remote(x_ref, x.at[block(d)], (p1, t))
    x2 = remote(x_ref, x.at[block(d)], (p2, t))
    gathered = [
        remote(g_ref, gz.at[q], (d, ((q + o) % nd) * k + m)) for o in range(1, nd)
    ]

    load_x.wait()
    u_part[t] = mm(down_ref[...], x[block(d)], 1, 1)

    load_w.wait()

    @pl.loop(0, rows // side)
    def _(i):
        r = pl.ds(pl.multiple_of(i * side, side), side)
        total = jnp.zeros((side, 128), f32)
        for c in range(n_tile):
            cols = slice(c * width, (c + 1) * width)
            merged = w[r, cols].astype(f32) + adapter_scale * mm(up_ref[r, :], down_ref[:, cols], 1, 0)
            w[r, cols] = merged.astype(bf16)
            square = merged * merged
            for lane in range(0, width, 128):
                total = total + square[:, lane:lane + 128]
        squares[t, :, r] = jnp.sum(total.T, axis=0, keepdims=True)

    squares_sent = share_out(squares)

    load_g.wait()
    for copy in gathered:
        copy.wait_recv()
    moved = [
        remote(gz.at[p], grad.at[m, block(d)], (p, t)) for p in (p3, p1, p2)
    ]
    keep_g = pltpu.make_async_copy(gz.at[d], grad.at[m, block(d)], local_sem.at[3])
    keep_g.start()
    u_sent = share_out(u_part)

    def near(source):
        return [
            remote(grad.at[m, block(source)], grad.at[m, block(source)], (d, q * k + (m + o) % k))
            for o in range(1, k)
        ]

    for copy in squares_sent:
        copy.wait_recv()
    total = squares[0]
    for i in range(1, nt):
        total = total + squares[i]
    norm = jnp.sqrt(total + epsilon)
    scale = mag_ref[...] / norm

    keep_g.wait()
    swapped = {0: near(d)}
    x1.wait_recv()
    x2.wait_recv()
    for s, copy, p in zip((3, 1, 2), moved, (p3, p1, p2)):
        copy.wait_recv()
        swapped[s] = near(p)
    x3 = remote(x.at[block(p1, half)], x.at[block(p1, half)], (p2, t))
    x4 = remote(x.at[block(p2, half, half)], x.at[block(p2, half, half)], (p1, t))

    def share(s, p):
        for copy in swapped[s]:
            copy.wait_recv()
        at = block(p)
        for j in range(k):
            scaled[j, at] = (grad[j, at].astype(f32) * scale[:, j * nr:(j + 1) * nr]).astype(bf16)

        @pl.loop(0, n_tile)
        def _(i):
            cols = pl.ds(pl.multiple_of(i * width, width), width)
            acc = mm(scaled[0, at], w[0:nr, cols], 1, 0)
            for j in range(1, k):
                acc = acc + mm(scaled[j, at], w[j * nr:(j + 1) * nr, cols], 1, 0)
            if s:
                part[s - 1, :, cols] = acc.astype(bf16)
            else:
                own[:, cols] = acc

    low, high = pl.ds(0, half), pl.ds(half, half)
    share(3, p3)
    a1 = remote(part.at[2, low], got.at[0], (p1, t))
    b1 = remote(part.at[2, high], got.at[1], (p2, t))
    share(1, p1)
    a2 = remote(part.at[0, low], got.at[2], (p1, t))
    share(2, p2)
    b2 = remote(part.at[1, high], got.at[3], (p2, t))
    share(0, d)

    total = mm(upt_ref[:, 0:nr], scaled[0], 1, 1)
    for j in range(1, k):
        total = total + mm(upt_ref[:, j * nr:(j + 1) * nr], scaled[j], 1, 1)
    v[d] = total.astype(bf16)
    lanes = pl.ds(pl.multiple_of(m * (nd * tokens // k), 128), nd * tokens // k)
    v_moved = [remote(v.at[d, :, lanes], v.at[d, :, lanes], (p, t)) for p in (p1, p2, p3)]

    for copy in u_sent:
        copy.wait_recv()
    total = u_part[0]
    for i in range(1, nt):
        total = total + u_part[i]
    u[d] = total.astype(bf16)
    u_moved = [remote(u.at[d], u.at[d], (p, t)) for p in (p1, p2, p3)]

    def combine(copy, slot, index, at):
        copy.wait_recv()

        @pl.loop(0, n_tile)
        def _(i):
            cols = pl.ds(pl.multiple_of(i * width, width), width)
            part[index, at, cols] = (
                part[index, at, cols].astype(f32) + got[slot, :, cols].astype(f32)
            ).astype(bf16)

    x3.wait_recv()
    x4.wait_recv()

    def row_sums(j):
        @pl.loop(0, nr // side)
        def _(i):
            r = pl.ds(pl.multiple_of(j * nr + i * side, side), side)
            inner = pl.ds(pl.multiple_of(i * side, side), side)
            y = mm(x[...], w[r, :], 1, 1)
            sums[t, :, r] = jnp.sum(y * grad[j, :, inner].astype(f32), axis=0, keepdims=True)

    for j in range(k // 2):
        row_sums(j)
    combine(a1, 0, 1, low)
    a3 = remote(part.at[1, low], got.at[4], (p2, t))
    combine(b1, 1, 0, high)
    b3 = remote(part.at[0, high], got.at[5], (p1, t))
    for j in range(k // 2, k):
        row_sums(j)
    sums_sent = share_out(sums)

    for copy in u_moved:
        copy.wait_recv()
    for j in range(k):
        total = mm(u[0], grad[j, 0:tokens], 1, 0)
        for b in range(1, nd):
            total = total + mm(u[b], grad[j, b * tokens:(b + 1) * tokens], 1, 0)
        at = slice(j * nr, (j + 1) * nr)
        ug_ref[:, at] = adapter_scale * scale[:, at] * total

    for copy in v_moved:
        copy.wait_recv()
    total = v[0, :, lanes].astype(f32)
    for b in range(1, nd):
        total = total + v[b, :, lanes].astype(f32)
    v_all[:, lanes] = total.astype(bf16)
    v_near = [
        remote(v_all.at[:, lanes], v_all.at[:, lanes], (d, q * k + (m + o) % k))
        for o in range(1, k)
    ]
    for copy in v_near:
        copy.wait_recv()
    for c in range(n_tile):
        cols = slice(c * width, (c + 1) * width)
        dg_ref[:, cols] = adapter_scale * mm(v_all[...], x[:, cols], 1, 0)

    for copy in sums_sent:
        copy.wait_recv()
    total = sums[0]
    for i in range(1, nt):
        total = total + sums[i]
    mg_ref[...] = total / norm

    def finish(second, third, i2, i3, at):
        second.wait_recv()
        third.wait_recv()

        @pl.loop(0, n_tile)
        def _(i):
            cols = pl.ds(pl.multiple_of(i * width, width), width)
            dx_ref[at, cols] = (
                own[at, cols] + got[i2, :, cols].astype(f32) + got[i3, :, cols].astype(f32)
            ).astype(bf16)

    finish(a2, a3, 2, 4, low)
    finish(b2, b3, 3, 5, high)
    for copy in started:
        copy.wait_send()
    assert used[0] == n_local, used[0]


def local(inputs, output_gradient, frozen, down, up, magnitude):
    nd, nt = lax.axis_size("dp"), lax.axis_size("tensor")
    k = nt // nd
    tokens, columns = inputs.shape
    rows = frozen.shape[0]
    rank = down.shape[0]
    nr = output_gradient.shape[1]
    n_copies = 2 + (nd - 1) + 3 * (nt - 1) + 3 * 3 + (nd + 1) * (k - 1) + 2 + 6
    anywhere = pl.BlockSpec(memory_space=pl.ANY)
    vmem = pl.BlockSpec(memory_space=pltpu.VMEM)
    half = tokens // 2
    dx, dg, ug, mg = pl.pallas_call(
        functools.partial(kernel, nd, nt, n_copies),
        out_shape=(
            jax.ShapeDtypeStruct((tokens, columns), bf16),
            jax.ShapeDtypeStruct((rank, columns), f32),
            jax.ShapeDtypeStruct((rank, rows), f32),
            jax.ShapeDtypeStruct((1, rows), f32),
        ),
        in_specs=[anywhere] * 3 + [vmem] * 4,
        out_specs=(vmem,) * 4,
        scratch_shapes=[
            pltpu.VMEM((rows, columns), bf16),
            pltpu.VMEM((nd * tokens, columns), bf16),
            pltpu.VMEM((nd, tokens, nr), bf16),
            pltpu.VMEM((k, nd * tokens, nr), bf16),
            pltpu.VMEM((k, nd * tokens, nr), bf16),
            pltpu.VMEM((3, tokens, columns), bf16),
            pltpu.VMEM((tokens, columns), f32),
            pltpu.VMEM((6, half, columns), bf16),
            pltpu.VMEM((nt, rank, tokens), f32),
            pltpu.VMEM((nd, rank, tokens), bf16),
            pltpu.VMEM((nd, rank, nd * tokens), bf16),
            pltpu.VMEM((rank, nd * tokens), bf16),
            pltpu.VMEM((nt, 1, rows), f32),
            pltpu.VMEM((nt, 1, rows), f32),
            pltpu.SemaphoreType.DMA((n_copies,)),
            pltpu.SemaphoreType.DMA((n_copies,)),
            pltpu.SemaphoreType.DMA((4,)),
        ],
        compiler_params=pltpu.CompilerParams(
            collective_id=0, has_side_effects=True, vmem_limit_bytes=62 * 1024 * 1024
        ),
    )(inputs, output_gradient, frozen, down, up, up.T, magnitude[None, :])
    return dx, dg, ug.T, mg[0]


def solution(mesh):
    placed = (
        P("dp", "tensor"),
        P("dp", "tensor"),
        P("dp", "tensor"),
        P(None, "tensor"),
        P("dp", None),
        P("dp"),
    )
    return jax.shard_map(
        local,
        mesh=mesh,
        in_specs=placed,
        out_specs=(P("dp", "tensor"), P(None, "tensor"), P("dp", None), P("dp")),
        check_vma=False,
    )
```
